512 devices in a mesh: dp: 64 (over x, y_lo, z), tensor: 8 (over y_hi, core).
Axes of the slice: x: 4, y: 8 (y_hi: 4, y_lo: 2; y = y_hi * 2 + y_lo), z: 8, core: 2. Of those that a mesh axis runs over, the one named last changes fastest.
Arguments:
- tokens: bfloat16 [32768, 1024], P('dp', 'tensor'), may hold values from -6 to 6
- cotangent: bfloat16 [32768, 1024], P('dp', 'tensor'), may hold values from -6 to 6
- w_in: bfloat16 [4096, 1024], P(('dp', 'tensor')), may hold values from -0.1875 to 0.1875
- b_in: bfloat16 [4096], P(('dp', 'tensor')), may hold values from -4 to 4
- w_out: bfloat16 [4096, 1024], P(('dp', 'tensor')), may hold values from -0.09375 to 0.09375
Outputs:
- mixed: bfloat16 [32768, 1024], P('dp', 'tensor')
- grad_in: float32 [4096, 1024], P(('dp', 'tensor'))
The draws below stay inside these ranges and needn't reach their ends.
All inputs are finite; a program needn't handle non-finite values.
Results may differ from the reference program's by a relative error of at most 0.017.
Values may be sent and summed in bfloat16 or wider, within the bound.
A program may use at most 64 MiB of HBM per device.

```python
import math
import jax
import jax.numpy as jnp
from jax import lax

D = 1024
FF = 4096
TOKENS = 32768
N_DP = 64
N_TENSOR = 8


def levels(key, shape, split, low, largest):
    level = 1.0
    for axis_at, shards_of in split:
        heights = jax.random.uniform(jax.random.fold_in(jax.random.fold_in(key, 6), axis_at), (shards_of,), jnp.float32, low / len(split), largest / len(split))
        level = level * jnp.repeat(jnp.exp(heights), shape[axis_at] // shards_of).reshape((-1,) + (1,) * (len(shape) - 1 - axis_at))
    return level


def normal_values(rng, dims, deviation, most, pieces=(), held_as=jnp.bfloat16):
    drawn = deviation * jax.random.normal(rng, dims, jnp.float32)
    if pieces:
        drawn = drawn * levels(rng, dims, pieces, -0.22, 0.18)
    return jnp.clip(drawn, -most, most).astype(held_as)


def setup_inputs(seed: int = 0) -> dict:
    keys = jax.random.split(jax.random.key(seed), 6)
    return {
        "tokens": normal_values(keys[0], (TOKENS, D), 1.0, 6.0, ((0, 64), (1, 8))),
        "cotangent": normal_values(keys[1], (TOKENS, D), 1.0, 6.0, ((0, 64), (1, 8))),
        "w_in": normal_values(keys[2], (FF, D), D ** -0.5, 0.1875, ((0, 512),)),
        "b_in": normal_values(keys[3], (FF,), 1.0, 4.0, ((0, 512),)),
        "w_out": normal_values(keys[4], (FF, D), FF ** -0.5, 0.09375, ((0, 512),)),
    }


def gelu_parts(value):
    coeff = 0.7978845608
    inner = coeff * (value + 0.044715 * value * value * value)
    tangent = jnp.tanh(inner)
    result = 0.5 * value * (1.0 + tangent)
    slope = 0.5 * (1.0 + tangent) + 0.5 * value * (1.0 - tangent * tangent) * coeff * (1.0 + 3.0 * 0.044715 * value * value)
    return (result, slope)

def reference(tokens, cotangent, w_in, b_in, w_out):
    contract_last = (((1,), (1,)), ((), ()))
    contract_first = (((0,), (0,)), ((), ()))
    owned = FF // (N_TENSOR * N_DP)
    units = FF // N_TENSOR
    in_groups = w_in.reshape(N_DP, N_TENSOR, owned, D).transpose(1, 0, 2, 3).reshape(N_TENSOR, units, D)
    out_groups = w_out.reshape(N_DP, N_TENSOR, owned, D).transpose(1, 0, 2, 3).reshape(N_TENSOR, units, D)
    bias_groups = b_in.reshape(N_DP, N_TENSOR, owned).transpose(1, 0, 2).reshape(N_TENSOR, units)

    def step(total, items):
        in_rows, bias_rows, out_rows = items
        pre = lax.dot_general(tokens, in_rows, contract_last, preferred_element_type=jnp.float32) + bias_rows.astype(jnp.float32)
        act_value, slope = gelu_parts(pre)
        act = act_value.astype(jnp.bfloat16)
        part = jnp.dot(act, out_rows, preferred_element_type=jnp.float32).astype(jnp.bfloat16)
        part = lax.optimization_barrier(part).astype(jnp.float32)
        dact = lax.dot_general(cotangent, out_rows, contract_last, preferred_element_type=jnp.float32)
        dpre = (dact * slope).astype(jnp.bfloat16)
        grad = lax.dot_general(dpre, tokens, contract_first, preferred_element_type=jnp.float32)
        return (total + part, grad)
    total, grads = lax.scan(step, jnp.zeros((TOKENS, D), jnp.float32), (in_groups, bias_groups, out_groups))
    grad_in = grads.reshape(N_TENSOR, N_DP, owned, D).transpose(1, 0, 2, 3).reshape(FF, D)
    grad_in = grad_in * (1.0 / math.sqrt(TOKENS))
    return (total.astype(jnp.bfloat16), grad_in)
```

```python
import math

import jax
import jax.numpy as jnp
from jax import lax
from jax.experimental import pallas as pl
from jax.experimental.pallas import tpu as pltpu
from jax.sharding import PartitionSpec as P

MESH = pl.DeviceIdType.MESH
BF16, F32 = jnp.bfloat16, jnp.float32
NX, NL, NZ, NY = 4, 2, 8, 4
ROWS, D, OWN = 512, 1024, 8
UNITS = NX * NL * NZ * OWN
BW = D + 128
HALF = ROWS // 2


def gelu_parts(value):
    coeff = 0.7978845608
    square = value * value
    tangent = jnp.tanh(coeff * value * (1.0 + 0.044715 * square))
    half = 0.5 * (1.0 + tangent)
    slope = half + 0.5 * value * (1.0 - tangent * tangent) * coeff * (1.0 + 3.0 * 0.044715 * square)
    return value * half, slope


def kernel(
    tok_in, cot_in, win_in, b_in, wout_in, mixed_out, grad_out,
    tok, cot, w_i, w_o, act, slope, dpre, mix_s, mix_r, mix_o, mix_in, g_s, g_r, g_p, g_q,
    send_sem, recv_sem,
):
    d, t = lax.axis_index("dp"), lax.axis_index("tensor")
    x, yl, z = d // (NL * NZ), (d // NZ) % NL, d % NZ
    yh, c = t // 2, t % 2

    def peer(dx=0, dl=0, dz=0, dy=0, dc=0):
        px, pz, py = (x + dx + NX) % NX, (z + dz + NZ) % NZ, (yh + dy + NY) % NY
        return ((px * NL + (yl + dl) % NL) * NZ + pz, py * 2 + (c + dc) % 2)

    count = [0]
    started = []

    def send(src, dst, to):
        k = count[0]
        count[0] += 1
        copy = pltpu.make_async_remote_copy(
            src_ref=src, dst_ref=dst, send_sem=send_sem.at[k], recv_sem=recv_sem.at[k],
            device_id=to, device_id_type=MESH,
        )
        copy.start()
        started.append(copy)
        return copy

    near_x = [dict(dx=i) for i in (2, 1, -1)]
    near_lz = [dict(dz=i, dl=l) for i in (4, 3, -3, 2, -2, 1, -1, 0) for l in (1, 0) if (i, l) != (0, 0)]
    near_xl = [dict(dx=i, dl=l) for i in (2, 1, -1, 0) for l in (1, 0) if (i, l) != (0, 0)]
    near_y = [dict(dy=i) for i in (2, 1, -1)]
    sibling = dict(dc=1)

    barrier = pltpu.get_barrier_semaphore()
    greeted = near_lz + near_x + [p for p in near_xl if p.get("dl") and p.get("dx")] + near_y + [sibling]
    for p in greeted:
        pl.semaphore_signal(barrier, inc=1, device_id=peer(**p), device_id_type=MESH)

    own_columns = pl.ds(pl.multiple_of(t * 128, 128), 128)
    tok[:, own_columns] = tok_in[...]
    cot[:, own_columns] = cot_in[...]
    eye = lax.broadcasted_iota(jnp.int32, (OWN, OWN), 0) == lax.broadcasted_iota(jnp.int32, (OWN, OWN), 1)
    bias = jnp.broadcast_to(b_in[...].astype(F32), (OWN, OWN))
    bias = jnp.sum(jnp.where(eye, bias, 0.0), axis=1, keepdims=True)
    w_i[x, yl, z, :, 0:D] = win_in[...]
    w_i[x, yl, z, :, D:BW] = jnp.broadcast_to(bias, (OWN, 128)).astype(BF16)
    w_o[x, yl, z] = wout_in[...]
    pl.semaphore_wait(barrier, len(greeted))

    def columns(dy, dc=0):
        py, pc = (yh + dy + NY) % NY, (c + dc) % 2
        return pl.ds(pl.multiple_of(py * 256 + pc * 128, 128), 128)

    top, bottom, whole = pl.ds(0, HALF), pl.ds(HALF, HALF), pl.ds(0, ROWS)

    def place(buf, rows, dy):
        return buf.at[rows, columns(dy)]

    def spread(buf):
        out = {}
        out["up_a"] = send(place(buf, top, 0), place(buf, top, 0), peer(dy=1))
        out["dn_b"] = send(place(buf, bottom, 0), place(buf, bottom, 0), peer(dy=-1))
        out["up_b"] = send(place(buf, bottom, 0), place(buf, bottom, 0), peer(dy=1))
        out["dn_a"] = send(place(buf, top, 0), place(buf, top, 0), peer(dy=-1))
        out["sib"] = [send(place(buf, whole, 0), place(buf, whole, 0), peer(**sibling))]
        return out

    def pass_on(buf, out):
        out["up_a"].wait_recv()
        out["fw_a"] = send(place(buf, top, -1), place(buf, top, -1), peer(dy=1))
        out["dn_b"].wait_recv()
        out["fw_b"] = send(place(buf, bottom, 1), place(buf, bottom, 1), peer(dy=-1))

    def share(buf, out, near):
        if near:
            for key, dy in (("up_b", -1), ("dn_a", 1)):
                out[key].wait_recv()
                out["sib"].append(send(place(buf, whole, dy), place(buf, whole, dy), peer(**sibling)))
        else:
            for key, rows in (("fw_a", top), ("fw_b", bottom)):
                out[key].wait_recv()
                out["sib"].append(send(place(buf, rows, 2), place(buf, rows, 2), peer(**sibling)))

    def settle(out):
        for copy in out["sib"]:
            copy.wait_recv()

    tok_moves = spread(tok)
    wo_first = [send(w_o.at[x, yl, z], w_o.at[x, yl, z], peer(**p)) for p in near_xl]
    wi_first = [send(w_i.at[x, yl, z], w_i.at[x, yl, z], peer(**p)) for p in near_lz]

    def ring_step(step):
        back, ahead = (z - step + 1 + NZ) % NZ, (z + step - 1) % NZ
        xs_up, xs_dn = pl.ds(0, NX), pl.ds(0, NX)
        if step == NZ // 2:
            xs_up, xs_dn = pl.ds(0, NX // 2), pl.ds(NX // 2, NX // 2)
        return [
            send(w_o.at[xs_up, :, back], w_o.at[xs_up, :, back], peer(dz=1)),
            send(w_o.at[xs_dn, :, ahead], w_o.at[xs_dn, :, ahead], peer(dz=-1)),
        ]

    def arrive(moves):
        for copy in moves:
            copy.wait_recv()

    arrive(wo_first)
    ring = ring_step(1)
    pass_on(tok, tok_moves)
    cot_moves = spread(cot)
    arrive(wi_first)
    wi_second = [send(w_i.at[x], w_i.at[x], peer(**p)) for p in near_x]
    share(tok, tok_moves, True)
    arrive(ring)
    ring = ring_step(2)
    share(tok, tok_moves, False)
    pass_on(cot, cot_moves)
    arrive(ring)
    ring = ring_step(3)
    arrive(wi_second)
    settle(tok_moves)

    def part(ref, j, width):
        value = ref[2 * j : 2 * j + 2].astype(F32)
        return value.reshape(UNITS // 2, width).astype(BF16)

    last = (((1,), (1,)), ((), ()))
    first = (((0,), (0,)), ((), ()))
    pick = (lax.broadcasted_iota(jnp.int32, (OWN, 128), 1) == 0).astype(F32).astype(BF16)
    for j in range(2):
        rows = part(w_i, j, BW)
        bias = lax.dot_general(pick, rows[:, D:BW], last, preferred_element_type=F32)
        pre = lax.dot_general(tok[...], rows[:, 0:D], last, preferred_element_type=F32) + bias[0:1, :]
        value, grade = gelu_parts(pre)
        act[:, j * 256 : (j + 1) * 256] = value.astype(BF16)
        slope[:, j * 256 : (j + 1) * 256] = grade
        if j == 0:
            arrive(ring)
            ring = ring_step(4)
            share(cot, cot_moves, True)
    arrive(ring)

    pair = []
    for k, dy in enumerate((2, 1, -1, 0)):
        span = pl.ds(pl.multiple_of(((yh + dy + NY) % NY) * 256, 256), 256)
        weights = w_o[:, :, :, :, span].astype(F32).reshape(UNITS, 256).astype(BF16)
        term = jnp.dot(act[...], weights, preferred_element_type=F32)
        mix_s[k] = term.astype(BF16)
        theirs = pl.ds(pl.multiple_of((1 - c) * 128, 128), 128)
        pair.append(send(mix_s.at[k, :, theirs], mix_r.at[k], peer(**sibling)))
    share(cot, cot_moves, False)
    mine = pl.ds(pl.multiple_of(c * 128, 128), 128)
    out_moves = []
    for k, p in enumerate(near_y):
        pair[k].wait_recv()
        mix_o[k] = (mix_s[k, :, mine].astype(F32) + mix_r[k].astype(F32)).astype(BF16)
        out_moves.append(send(mix_o.at[k], mix_in.at[k], peer(**p)))
    settle(cot_moves)

    for j in range(2):
        dact = lax.dot_general(cot[...], part(w_o, j, D), last, preferred_element_type=F32)
        cols = slice(j * 256, (j + 1) * 256)
        dpre[:, cols] = (dact * slope[:, cols]).astype(BF16)

    def grads(px):
        units = pl.ds(pl.multiple_of(px * 128, 128), 128)
        return lax.dot_general(dpre[:, units], tok[...], first, preferred_element_type=F32).reshape(NL, NZ, OWN, D)

    x_moves = []
    for k, p in enumerate(near_x):
        g_s[k] = grads((x + p["dx"] + NX) % NX).astype(BF16)
        x_moves.append(send(g_s.at[k], g_r.at[k], peer(**p)))
    total = grads(x)

    pair[3].wait_recv()
    result = mix_s[3, :, mine].astype(F32) + mix_r[3].astype(F32)
    for k in range(3):
        out_moves[k].wait_recv()
        result = result + mix_in[k].astype(F32)
    mixed_out[...] = result.astype(BF16)

    arrive(x_moves)
    total = total + (g_r[0].astype(F32) + g_r[1].astype(F32) + g_r[2].astype(F32))
    g_p[...] = total.astype(BF16)
    lz_moves = []
    for k, p in enumerate(near_lz):
        block = g_p.at[(yl + p["dl"]) % NL, (z + p["dz"] + NZ) % NZ]
        lz_moves.append(send(block, g_q.at[k], peer(**p)))
    total = g_p[yl, z].astype(F32)
    for k in range(len(near_lz)):
        lz_moves[k].wait_recv()
        total = total + g_q[k].astype(F32)
    grad_out[...] = total * (1.0 / math.sqrt(ROWS * NX * NL * NZ))

    for copy in started:
        copy.wait_send()


def on_device(tokens, cotangent, w_in, b_in, w_out):
    vmem = pl.BlockSpec(memory_space=pltpu.VMEM)
    return pl.pallas_call(
        kernel,
        out_shape=(
            jax.ShapeDtypeStruct((ROWS, 128), BF16),
            jax.ShapeDtypeStruct((OWN, D), F32),
        ),
        in_specs=[vmem] * 5,
        out_specs=(vmem, vmem),
        scratch_shapes=[
            pltpu.VMEM((ROWS, D), BF16),
            pltpu.VMEM((ROWS, D), BF16),
            pltpu.VMEM((NX, NL, NZ, OWN, BW), BF16),
            pltpu.VMEM((NX, NL, NZ, OWN, D), BF16),
            pltpu.VMEM((ROWS, UNITS), BF16),
            pltpu.VMEM((ROWS, UNITS), F32),
            pltpu.VMEM((ROWS, UNITS), BF16),
            pltpu.VMEM((4, ROWS, 256), BF16),
            pltpu.VMEM((4, ROWS, 128), BF16),
            pltpu.VMEM((3, ROWS, 128), BF16),
            pltpu.VMEM((3, ROWS, 128), BF16),
            pltpu.VMEM((3, NL, NZ, OWN, D), BF16),
            pltpu.VMEM((3, NL, NZ, OWN, D), BF16),
            pltpu.VMEM((NL, NZ, OWN, D), BF16),
            pltpu.VMEM((NL * NZ - 1, OWN, D), BF16),
            pltpu.SemaphoreType.DMA((90,)),
            pltpu.SemaphoreType.DMA((90,)),
        ],
        compiler_params=pltpu.CompilerParams(
            collective_id=0, has_side_effects=True, vmem_limit_bytes=48 * 1024 * 1024
        ),
        cost_estimate=pl.CostEstimate(flops=2147483648, bytes_accessed=8388608, transcendentals=262144),
    )(tokens, cotangent, w_in, b_in.reshape(1, OWN), w_out)


def solution(mesh):
    in_specs = (
        P("dp", "tensor"),
        P("dp", "tensor"),
        P(("dp", "tensor"), None),
        P(("dp", "tensor")),
        P(("dp", "tensor"), None),
    )
    out_specs = (P("dp", "tensor"), P(("dp", "tensor"), None))
    return jax.shard_map(
        on_device, mesh=mesh, in_specs=in_specs, out_specs=out_specs, check_vma=False
    )
```

```python
import math

import jax
import jax.numpy as jnp
from jax import lax
from jax.experimental import pallas as pl
from jax.experimental.pallas import tpu as pltpu
from jax.sharding import PartitionSpec as P

MESH = pl.DeviceIdType.MESH
BF16, F32 = jnp.bfloat16, jnp.float32
NX, NL, NZ, NY = 4, 2, 8, 4
ROWS, D, OWN = 512, 1024, 8
UNITS = NX * NL * NZ * OWN
BW = D + 128
HALF = ROWS // 2
CX = 768


def gelu_parts(value):
    coeff = 0.7978845608
    square = value * value
    tangent = jnp.tanh(coeff * value * (1.0 + 0.044715 * square))
    half = 0.5 * (1.0 + tangent)
    slope = half + 0.5 * value * (1.0 - tangent * tangent) * coeff * (1.0 + 3.0 * 0.044715 * square)
    return value * half, slope


def kernel(
    tok_in, cot_in, win_in, b_in, wout_in, mixed_out, grad_out,
    tok, cot, w_i, w_o, b_own, act, slope, dpre, mix_s, mix_r, mix_o, mix_in,
    g_s, g_r, g_p, g_q, h_s, h_r, h_p, h_q,
    send_sem, recv_sem, local_sem,
):
    d, t = lax.axis_index("dp"), lax.axis_index("tensor")
    x, yl, z = d // (NL * NZ), (d // NZ) % NL, d % NZ
    yh, c = t // 2, t % 2

    def peer(dx=0, dl=0, dz=0, dy=0, dc=0):
        px, pz, py = (x + dx + NX) % NX, (z + dz + NZ) % NZ, (yh + dy + NY) % NY
        return ((px * NL + (yl + dl) % NL) * NZ + pz, py * 2 + (c + dc) % 2)

    count = [0]
    started = []

    def send(src, dst, to):
        k = count[0]
        count[0] += 1
        copy = pltpu.make_async_remote_copy(
            src_ref=src, dst_ref=dst, send_sem=send_sem.at[k], recv_sem=recv_sem.at[k],
            device_id=to, device_id_type=MESH,
        )
        copy.start()
        started.append(copy)
        return copy

    near_x = [dict(dx=i) for i in (2, 1, -1)]
    near_z = [dict(dz=i) for i in (1, -1, 2, -2, 3, -3, 4)]
    near_xl = [dict(dx=i, dl=l) for i in (2, 1, -1, 0) for l in (1, 0) if (i, l) != (0, 0)]
    near_lz = [dict(dz=i, dl=l) for i in (4, 3, -3, 2, -2, 1, -1, 0) for l in (1, 0) if (i, l) != (0, 0)]
    near_y = [dict(dy=i) for i in (2, 1, -1)]
    sibling, partner = dict(dc=1), dict(dl=1)

    barrier = pltpu.get_barrier_semaphore()
    greeted = near_lz + [p for p in near_xl if p["dx"]] + near_y + [sibling]
    for p in greeted:
        pl.semaphore_signal(barrier, inc=1, device_id=peer(**p), device_id_type=MESH)

    own_columns = pl.ds(pl.multiple_of(t * 128, 128), 128)
    local = [
        pltpu.make_async_copy(src, dst, local_sem.at[k])
        for k, (src, dst) in enumerate((
            (b_in, b_own),
            (win_in, w_i.at[x, z, yl, :, pl.ds(0, D)]),
            (wout_in, w_o.at[z, yl, x]),
            (tok_in, tok.at[:, own_columns]),
            (cot_in, cot.at[:, own_columns]),
        ))
    ]
    for copy in local:
        copy.start()
    local[0].wait()
    eye = lax.broadcasted_iota(jnp.int32, (OWN, OWN), 0) == lax.broadcasted_iota(jnp.int32, (OWN, OWN), 1)
    bias = jnp.broadcast_to(b_own[...].astype(F32), (OWN, OWN))
    bias = jnp.sum(jnp.where(eye, bias, 0.0), axis=1, keepdims=True)
    w_i[x, z, yl, :, D:BW] = jnp.broadcast_to(bias, (OWN, 128)).astype(BF16)
    for copy in local[1:]:
        copy.wait()
    pl.semaphore_wait(barrier, len(greeted))

    def columns(dy, dc=0):
        py, pc = (yh + dy + NY) % NY, (c + dc) % 2
        return pl.ds(pl.multiple_of(py * 256 + pc * 128, 128), 128)

    top, bottom, whole = pl.ds(0, HALF), pl.ds(HALF, HALF), pl.ds(0, ROWS)

    def place(buf, rows, dy):
        return buf.at[rows, columns(dy)]

    def spread(buf):
        out = {}
        out["up_a"] = send(place(buf, top, 0), place(buf, top, 0), peer(dy=1))
        out["dn_b"] = send(place(buf, bottom, 0), place(buf, bottom, 0), peer(dy=-1))
        out["up_b"] = send(place(buf, bottom, 0), place(buf, bottom, 0), peer(dy=1))
        out["dn_a"] = send(place(buf, top, 0), place(buf, top, 0), peer(dy=-1))
        out["sib"] = [send(place(buf, whole, 0), place(buf, whole, 0), peer(**sibling))]
        return out

    def pass_on(buf, out):
        out["up_a"].wait_recv()
        out["fw_a"] = send(place(buf, top, -1), place(buf, top, -1), peer(dy=1))
        out["dn_b"].wait_recv()
        out["fw_b"] = send(place(buf, bottom, 1), place(buf, bottom, 1), peer(dy=-1))

    def share(buf, out, near):
        if near:
            for key, dy in (("up_b", -1), ("dn_a", 1)):
                out[key].wait_recv()
                out["sib"].append(send(place(buf, whole, dy), place(buf, whole, dy), peer(**sibling)))
        else:
            for key, rows in (("fw_a", top), ("fw_b", bottom)):
                out[key].wait_recv()
                out["sib"].append(send(place(buf, rows, 2), place(buf, rows, 2), peer(**sibling)))

    def settle(out):
        for copy in out["sib"]:
            copy.wait_recv()

    def arrive(moves):
        for copy in moves:
            copy.wait_recv()

    def wi_to_z(l):
        return [send(w_i.at[x, z, l], w_i.at[x, z, l], peer(**p)) for p in near_z]

    def wi_to_x(dz):
        pz = (z + dz + NZ) % NZ
        return [send(w_i.at[x, pz], w_i.at[x, pz], peer(**p)) for p in near_x]

    def wo_to_x(l):
        return [send(w_o.at[z, l, x], w_o.at[z, l, x], peer(**p)) for p in near_x]

    def ring_step(step, half, before=None):
        l = (yl + half) % NL
        out = []
        for k, sign in enumerate((1, -1)):
            if before is not None:
                before[k].wait_recv()
            if step < NZ // 2 or k == half:
                pz = (z - sign * (step - 1) + NZ) % NZ
                out.append(send(w_o.at[pz, l], w_o.at[pz, l], peer(dz=sign)))
        return out

    tok_moves = spread(tok)
    wi_own = send(w_i.at[x, z, yl], w_i.at[x, z, yl], peer(**partner))
    wo_own = send(w_o.at[z, yl, x], w_o.at[z, yl, x], peer(**partner))
    wo_moves = wo_to_x(yl)
    wi_moves = wi_to_z(yl)
    wi_own.wait_recv()
    wi_more = wi_to_z(1 - yl)
    wi_second = wi_to_x(0)
    wo_own.wait_recv()
    wo_more = wo_to_x(1 - yl)

    def relay(*dzs):
        out = []
        for dz in dzs:
            k = [p["dz"] for p in near_z].index(-dz if dz != 4 else 4)
            wi_moves[k].wait_recv()
            wi_more[k].wait_recv()
            out += wi_to_x(dz)
        return out

    arrive(wo_moves)
    ring = [ring_step(1, 0)]
    wi_second += relay(1, -1)
    arrive(wo_more)
    ring.append(ring_step(1, 1))
    pass_on(tok, tok_moves)
    cot_moves = spread(cot)
    wi_second += relay(2, -2)
    ring = [ring_step(2, h, ring[h]) for h in (0, 1)]
    wi_second += relay(3, -3, 4)
    share(tok, tok_moves, True)
    ring = [ring_step(3, h, ring[h]) for h in (0, 1)]
    share(tok, tok_moves, False)
    pass_on(cot, cot_moves)
    ring = [ring_step(4, h, ring[h]) for h in (0, 1)]
    arrive(wi_second)
    settle(tok_moves)

    last = (((1,), (1,)), ((), ()))

    def rows_of(value):
        return value.astype(F32).reshape(-1, value.shape[-1]).astype(BF16)

    for j in range(2):
        rows = rows_of(w_i[2 * j : 2 * j + 2])
        bias = rows[:, D:BW].astype(F32)
        pre = lax.dot_general(rows[:, 0:D], tok[...], last, preferred_element_type=F32)
        pre = pre + jnp.concatenate([bias] * (ROWS // 128), axis=1)
        value, grade = gelu_parts(pre)
        act[:, j * 256 : (j + 1) * 256] = value.astype(BF16).T
        slope[2 * j] = grade[0:128]
        slope[2 * j + 1] = grade[128:256]
        if j == 0:
            share(cot, cot_moves, True)
    arrive(ring[0] + ring[1])
    share(cot, cot_moves, False)
    settle(cot_moves)

    def units_of(px):
        dact = lax.dot_general(rows_of(w_o[:, :, px]), cot[...], last, preferred_element_type=F32)
        value = (dact * slope[px]).astype(BF16)
        dpre[px] = value
        return jnp.dot(value, tok[:, 0:CX], preferred_element_type=F32).reshape(NZ, NL, OWN, CX)

    x_moves = []
    for k, p in enumerate(near_x):
        g_s[k] = units_of((x + p["dx"] + NX) % NX).astype(BF16)
        x_moves.append(send(g_s.at[k], g_r.at[k], peer(**p)))
    total = units_of(x)
    rest = jnp.dot(dpre[...].reshape(UNITS, ROWS), tok[:, CX:D], preferred_element_type=F32)
    for px in range(NX):
        h_s[:, px] = rest[px * 128 : (px + 1) * 128].reshape(NZ, NL, OWN, D - CX).astype(BF16)
    far_z = near_z[::-1]
    z_moves = [send(h_s.at[(z + p["dz"] + NZ) % NZ], h_r.at[k], peer(**p)) for k, p in enumerate(far_z)]

    pair = []
    for k, dy in enumerate((2, 1, -1, 0)):
        span = pl.ds(pl.multiple_of(((yh + dy + NY) % NY) * 256, 256), 256)
        weights = jnp.concatenate([rows_of(w_o[:, :, px, :, span]) for px in range(NX)], axis=0)
        term = jnp.dot(act[...], weights, preferred_element_type=F32)
        mix_s[k] = term.astype(BF16)
        theirs = pl.ds(pl.multiple_of((1 - c) * 128, 128), 128)
        pair.append(send(mix_s.at[k, :, theirs], mix_r.at[k], peer(**sibling)))
    mine = pl.ds(pl.multiple_of(c * 128, 128), 128)
    out_moves = []
    for k, p in enumerate(near_y):
        pair[k].wait_recv()
        mix_o[k] = (mix_s[k, :, mine].astype(F32) + mix_r[k].astype(F32)).astype(BF16)
        out_moves.append(send(mix_o.at[k], mix_in.at[k], peer(**p)))

    arrive(x_moves)
    total = total + (g_r[0].astype(F32) + g_r[1].astype(F32) + g_r[2].astype(F32))
    g_p[...] = total.astype(BF16)
    lz_moves = []
    for k, p in enumerate(near_lz):
        block = g_p.at[(z + p["dz"] + NZ) % NZ, (yl + p["dl"]) % NL]
        lz_moves.append(send(block, g_q.at[k], peer(**p)))

    side = h_s[z].astype(F32)
    for k, copy in enumerate(z_moves):
        copy.wait_recv()
        side = side + h_r[k].astype(F32)
    h_p[...] = side.astype(BF16)
    xl_moves = []
    for k, p in enumerate(near_xl):
        block = h_p.at[(x + p["dx"] + NX) % NX, (yl + p["dl"]) % NL]
        xl_moves.append(send(block, h_q.at[k], peer(**p)))

    pair[3].wait_recv()
    result = mix_s[3, :, mine].astype(F32) + mix_r[3].astype(F32)
    for k in range(3):
        out_moves[k].wait_recv()
        result = result + mix_in[k].astype(F32)
    mixed_out[...] = result.astype(BF16)

    scale = 1.0 / math.sqrt(ROWS * NX * NL * NZ)
    total = h_p[x, yl].astype(F32)
    for k in range(len(near_xl)):
        xl_moves[k].wait_recv()
        total = total + h_q[k].astype(F32)
    grad_out[:, CX:D] = total * scale
    total = g_p[z, yl].astype(F32)
    for k in range(len(near_lz)):
        lz_moves[k].wait_recv()
        total = total + g_q[k].astype(F32)
    grad_out[:, 0:CX] = total * scale

    for copy in started:
        copy.wait_send()


def on_device(tokens, cotangent, w_in, b_in, w_out):
    vmem = pl.BlockSpec(memory_space=pltpu.VMEM)
    return pl.pallas_call(
        kernel,
        out_shape=(
            jax.ShapeDtypeStruct((ROWS, 128), BF16),
            jax.ShapeDtypeStruct((OWN, D), F32),
        ),
        in_specs=[pl.BlockSpec(memory_space=pltpu.HBM)] * 5,
        out_specs=(vmem, vmem),
        scratch_shapes=[
            pltpu.VMEM((ROWS, D), BF16),
            pltpu.VMEM((ROWS, D), BF16),
            pltpu.VMEM((NX, NZ, NL, OWN, BW), BF16),
            pltpu.VMEM((NZ, NL, NX, OWN, D), BF16),
            pltpu.VMEM((1, OWN), BF16),
            pltpu.VMEM((ROWS, UNITS), BF16),
            pltpu.VMEM((NX, UNITS // NX, ROWS), F32),
            pltpu.VMEM((NX, UNITS // NX, ROWS), BF16),
            pltpu.VMEM((4, ROWS, 256), BF16),
            pltpu.VMEM((4, ROWS, 128), BF16),
            pltpu.VMEM((3, ROWS, 128), BF16),
            pltpu.VMEM((3, ROWS, 128), BF16),
            pltpu.VMEM((3, NZ, NL, OWN, CX), BF16),
            pltpu.VMEM((3, NZ, NL, OWN, CX), BF16),
            pltpu.VMEM((NZ, NL, OWN, CX), BF16),
            pltpu.VMEM((NL * NZ - 1, OWN, CX), BF16),
            pltpu.VMEM((NZ, NX, NL, OWN, D - CX), BF16),
            pltpu.VMEM((NZ - 1, NX, NL, OWN, D - CX), BF16),
            pltpu.VMEM((NX, NL, OWN, D - CX), BF16),
            pltpu.VMEM((NX * NL - 1, OWN, D - CX), BF16),
            pltpu.SemaphoreType.DMA((150,)),
            pltpu.SemaphoreType.DMA((150,)),
            pltpu.SemaphoreType.DMA((5,)),
        ],
        compiler_params=pltpu.CompilerParams(
            collective_id=0, has_side_effects=True, vmem_limit_bytes=60 * 1024 * 1024
        ),
        cost_estimate=pl.CostEstimate(flops=2147483648, bytes_accessed=8388608, transcendentals=262144),
    )(tokens, cotangent, w_in, b_in.reshape(1, OWN), w_out)


def solution(mesh):
    in_specs = (
        P("dp", "tensor"),
        P("dp", "tensor"),
        P(("dp", "tensor"), None),
        P(("dp", "tensor")),
        P(("dp", "tensor"), None),
    )
    out_specs = (P("dp", "tensor"), P(("dp", "tensor"), None))
    return jax.shard_map(
        on_device, mesh=mesh, in_specs=in_specs, out_specs=out_specs, check_vma=False
    )
```

```python
import math

import jax
import jax.numpy as jnp
from jax import lax
from jax.experimental import pallas as pl
from jax.experimental.pallas import tpu as pltpu
from jax.sharding import PartitionSpec as P

MESH = pl.DeviceIdType.MESH
BF16, F32 = jnp.bfloat16, jnp.float32
NX, NL, NZ, NY = 4, 2, 8, 4
ROWS, D, OWN = 512, 1024, 8
UNITS = NX * NL * NZ * OWN
BW = D + 128
HALF = ROWS // 2
CX = 768


def gelu_parts(value):
    coeff = 0.7978845608
    square = value * value
    tangent = jnp.tanh(coeff * value * (1.0 + 0.044715 * square))
    half = 0.5 * (1.0 + tangent)
    slope = half + 0.5 * value * (1.0 - tangent * tangent) * coeff * (1.0 + 3.0 * 0.044715 * square)
    return value * half, slope


def kernel(
    tok_in, cot_in, win_in, b_in, wout_in, mixed_out, grad_out,
    tok, cot, w_i, w_o, b_own, act, slope, dpre, mix_s, mix_r, mix_o, mix_in,
    g_s, g_r, g_p, g_q, h_s, h_r, h_p, h_q,
    send_sem, recv_sem, local_sem,
):
    d, t = lax.axis_index("dp"), lax.axis_index("tensor")
    x, yl, z = d // (NL * NZ), (d // NZ) % NL, d % NZ
    yh, c = t // 2, t % 2

    def peer(dx=0, dl=0, dz=0, dy=0, dc=0):
        px, pz, py = (x + dx + NX) % NX, (z + dz + NZ) % NZ, (yh + dy + NY) % NY
        return ((px * NL + (yl + dl) % NL) * NZ + pz, py * 2 + (c + dc) % 2)

    count = [0]
    started = []

    def send(src, dst, to):
        k = count[0]
        count[0] += 1
        copy = pltpu.make_async_remote_copy(
            src_ref=src, dst_ref=dst, send_sem=send_sem.at[k], recv_sem=recv_sem.at[k],
            device_id=to, device_id_type=MESH,
        )
        copy.start()
        started.append(copy)
        return copy

    near_x = [dict(dx=i) for i in (2, 1, -1)]
    near_z = [dict(dz=i) for i in (1, -1, 2, -2, 3, -3, 4)]
    near_xl = [dict(dx=i, dl=l) for i in (2, 1, -1, 0) for l in (1, 0) if (i, l) != (0, 0)]
    near_lz = [dict(dz=i, dl=l) for i in (4, 3, -3, 2, -2, 1, -1, 0) for l in (1, 0) if (i, l) != (0, 0)]
    near_y = [dict(dy=i) for i in (2, 1, -1)]
    sibling, partner = dict(dc=1), dict(dl=1)

    barrier = pltpu.get_barrier_semaphore()
    greeted = near_lz + [p for p in near_xl if p["dx"]] + near_y + [sibling]
    for p in greeted:
        pl.semaphore_signal(barrier, inc=1, device_id=peer(**p), device_id_type=MESH)

    own_columns = pl.ds(pl.multiple_of(t * 128, 128), 128)
    local = [
        pltpu.make_async_copy(src, dst, local_sem.at[k])
        for k, (src, dst) in enumerate((
            (b_in, b_own),
            (win_in, w_i.at[x, z, yl, :, pl.ds(0, D)]),
            (wout_in, w_o.at[z, yl, x]),
            (tok_in, tok.at[:, own_columns]),
            (cot_in, cot.at[:, own_columns]),
        ))
    ]
    for copy in local:
        copy.start()
    local[0].wait()
    eye = lax.broadcasted_iota(jnp.int32, (OWN, OWN), 0) == lax.broadcasted_iota(jnp.int32, (OWN, OWN), 1)
    bias = jnp.broadcast_to(b_own[...].astype(F32), (OWN, OWN))
    bias = jnp.sum(jnp.where(eye, bias, 0.0), axis=1, keepdims=True)
    w_i[x, z, yl, :, D:BW] = jnp.broadcast_to(bias, (OWN, 128)).astype(BF16)
    for copy in local[1:]:
        copy.wait()
    pl.semaphore_wait(barrier, len(greeted))

    def columns(dy, dc=0):
        py, pc = (yh + dy + NY) % NY, (c + dc) % 2
        return pl.ds(pl.multiple_of(py * 256 + pc * 128, 128), 128)

    top, bottom, whole = pl.ds(0, HALF), pl.ds(HALF, HALF), pl.ds(0, ROWS)

    def place(buf, rows, dy):
        return buf.at[rows, columns(dy)]

    def spread(buf):
        out = {}
        out["up_a"] = send(place(buf, top, 0), place(buf, top, 0), peer(dy=1))
        out["dn_b"] = send(place(buf, bottom, 0), place(buf, bottom, 0), peer(dy=-1))
        out["up_b"] = send(place(buf, bottom, 0), place(buf, bottom, 0), peer(dy=1))
        out["dn_a"] = send(place(buf, top, 0), place(buf, top, 0), peer(dy=-1))
        out["sib"] = []
        return out

    def pass_on(buf, out):
        out["up_a"].wait_recv()
        out["fw_a"] = send(place(buf, top, -1), place(buf, top, -1), peer(dy=1))
        out["dn_b"].wait_recv()
        out["fw_b"] = send(place(buf, bottom, 1), place(buf, bottom, 1), peer(dy=-1))

    def share(buf, out, near):
        if near:
            for key, dy in (("up_b", -1), ("dn_a", 1)):
                out[key].wait_recv()
                out["sib"].append(send(place(buf, whole, dy), place(buf, whole, dy), peer(**sibling)))
        else:
            for key, rows in (("fw_a", top), ("fw_b", bottom)):
                out[key].wait_recv()
                out["sib"].append(send(place(buf, rows, 2), place(buf, rows, 2), peer(**sibling)))

    def settle(out):
        for copy in out["sib"]:
            copy.wait_recv()

    def arrive(moves):
        for copy in moves:
            copy.wait_recv()

    def wi_to_z(l):
        return [send(w_i.at[x, z, l], w_i.at[x, z, l], peer(**p)) for p in near_z]

    def wi_to_x(dz):
        pz = (z + dz + NZ) % NZ
        return [send(w_i.at[x, pz], w_i.at[x, pz], peer(**p)) for p in near_x]

    def wo_to_x(l):
        return [send(w_o.at[z, l, x], w_o.at[z, l, x], peer(**p)) for p in near_x]

    def ring_step(step, half, before=None):
        l = (yl + half) % NL
        out = []
        for k, sign in enumerate((1, -1)):
            if before is not None:
                before[k].wait_recv()
            if step < NZ // 2 or k == half:
                pz = (z - sign * (step - 1) + NZ) % NZ
                out.append(send(w_o.at[pz, l], w_o.at[pz, l], peer(dz=sign)))
        return out

    wi_own = send(w_i.at[x, z, yl], w_i.at[x, z, yl], peer(**partner))
    wo_own = send(w_o.at[z, yl, x], w_o.at[z, yl, x], peer(**partner))
    wo_moves = wo_to_x(yl)
    wi_moves = wi_to_z(yl)
    tok_moves = spread(tok)
    wi_own.wait_recv()
    wi_more = wi_to_z(1 - yl)
    wi_second = wi_to_x(0)
    wo_own.wait_recv()
    wo_more = wo_to_x(1 - yl)

    def relay(*dzs):
        out = []
        for dz in dzs:
            k = [p["dz"] for p in near_z].index(-dz if dz != 4 else 4)
            wi_moves[k].wait_recv()
            wi_more[k].wait_recv()
            out += wi_to_x(dz)
        return out

    arrive(wo_moves)
    ring = [ring_step(1, 0), None]
    wi_second += relay(1, -1)
    cot_moves = spread(cot)
    for buf, moves in ((tok, tok_moves), (cot, cot_moves)):
        moves['sib'].append(send(place(buf, whole, 0), place(buf, whole, 0), peer(**sibling)))
    arrive(wo_more)
    ring[1] = ring_step(1, 1)
    wi_second += relay(2, -2)
    ring[0] = ring_step(2, 0, ring[0])
    wi_second += relay(3, -3)
    wi_second += relay(4)
    ring[1] = ring_step(2, 1, ring[1])
    pass_on(tok, tok_moves)
    ring[0] = ring_step(3, 0, ring[0])
    ring[1] = ring_step(3, 1, ring[1])
    pass_on(cot, cot_moves)
    ring[0] = ring_step(4, 0, ring[0])
    ring[1] = ring_step(4, 1, ring[1])
    share(tok, tok_moves, True)
    share(tok, tok_moves, False)
    share(cot, cot_moves, True)
    arrive(wi_second)
    settle(tok_moves)

    last = (((1,), (1,)), ((), ()))

    def rows_of(value):
        return value.astype(F32).reshape(-1, value.shape[-1]).astype(BF16)

    for j in range(2):
        rows = rows_of(w_i[2 * j : 2 * j + 2])
        bias = rows[:, D:BW].astype(F32)
        pre = lax.dot_general(rows[:, 0:D], tok[...], last, preferred_element_type=F32)
        pre = pre + jnp.concatenate([bias] * (ROWS // 128), axis=1)
        value, grade = gelu_parts(pre)
        act[:, j * 256 : (j + 1) * 256] = value.astype(BF16).T
        slope[2 * j] = grade[0:128]
        slope[2 * j + 1] = grade[128:256]
    arrive(ring[0] + ring[1])
    pair = []
    for k, dy in enumerate((2, 1, -1, 0)):
        span = pl.ds(pl.multiple_of(((yh + dy + NY) % NY) * 256, 256), 256)
        weights = jnp.concatenate([rows_of(w_o[:, :, px, :, span]) for px in range(NX)], axis=0)
        term = jnp.dot(act[...], weights, preferred_element_type=F32)
        mix_s[k] = term.astype(BF16)
        theirs = pl.ds(pl.multiple_of((1 - c) * 128, 128), 128)
        pair.append(send(mix_s.at[k, :, theirs], mix_r.at[k], peer(**sibling)))
    share(cot, cot_moves, False)
    mine = pl.ds(pl.multiple_of(c * 128, 128), 128)
    out_moves = []
    for k, p in enumerate(near_y):
        pair[k].wait_recv()
        mix_o[k] = (mix_s[k, :, mine].astype(F32) + mix_r[k].astype(F32)).astype(BF16)
        out_moves.append(send(mix_o.at[k], mix_in.at[k], peer(**p)))
    settle(cot_moves)

    def units_of(px):
        dact = lax.dot_general(rows_of(w_o[:, :, px]), cot[...], last, preferred_element_type=F32)
        value = (dact * slope[px]).astype(BF16)
        dpre[px] = value
        return jnp.dot(value, tok[:, 0:CX], preferred_element_type=F32).reshape(NZ, NL, OWN, CX)

    x_moves = []
    for k, p in enumerate(near_x):
        g_s[k] = units_of((x + p["dx"] + NX) % NX).astype(BF16)
        x_moves.append(send(g_s.at[k], g_r.at[k], peer(**p)))
    total = units_of(x)
    rest = jnp.dot(dpre[...].reshape(UNITS, ROWS), tok[:, CX:D], preferred_element_type=F32)
    for px in range(NX):
        h_s[:, px] = rest[px * 128 : (px + 1) * 128].reshape(NZ, NL, OWN, D - CX).astype(BF16)
    far_z = near_z[::-1]
    z_moves = [send(h_s.at[(z + p["dz"] + NZ) % NZ], h_r.at[k], peer(**p)) for k, p in enumerate(far_z)]


    arrive(x_moves)
    total = total + (g_r[0].astype(F32) + g_r[1].astype(F32) + g_r[2].astype(F32))
    g_p[...] = total.astype(BF16)
    lz_moves = []
    for k, p in enumerate(near_lz):
        block = g_p.at[(z + p["dz"] + NZ) % NZ, (yl + p["dl"]) % NL]
        lz_moves.append(send(block, g_q.at[k], peer(**p)))

    side = h_s[z].astype(F32)
    for k, copy in enumerate(z_moves):
        copy.wait_recv()
        side = side + h_r[k].astype(F32)
    h_p[...] = side.astype(BF16)
    xl_moves = []
    for k, p in enumerate(near_xl):
        block = h_p.at[(x + p["dx"] + NX) % NX, (yl + p["dl"]) % NL]
        xl_moves.append(send(block, h_q.at[k], peer(**p)))

    pair[3].wait_recv()
    result = mix_s[3, :, mine].astype(F32) + mix_r[3].astype(F32)
    for k in range(3):
        out_moves[k].wait_recv()
        result = result + mix_in[k].astype(F32)
    mixed_out[...] = result.astype(BF16)

    scale = 1.0 / math.sqrt(ROWS * NX * NL * NZ)
    total = h_p[x, yl].astype(F32)
    for k in range(len(near_xl)):
        xl_moves[k].wait_recv()
        total = total + h_q[k].astype(F32)
    grad_out[:, CX:D] = total * scale
    total = g_p[z, yl].astype(F32)
    for k in range(len(near_lz)):
        lz_moves[k].wait_recv()
        total = total + g_q[k].astype(F32)
    grad_out[:, 0:CX] = total * scale

    for copy in started:
        copy.wait_send()


def on_device(tokens, cotangent, w_in, b_in, w_out):
    vmem = pl.BlockSpec(memory_space=pltpu.VMEM)
    return pl.pallas_call(
        kernel,
        out_shape=(
            jax.ShapeDtypeStruct((ROWS, 128), BF16),
            jax.ShapeDtypeStruct((OWN, D), F32),
        ),
        in_specs=[pl.BlockSpec(memory_space=pltpu.HBM)] * 5,
        out_specs=(vmem, vmem),
        scratch_shapes=[
            pltpu.VMEM((ROWS, D), BF16),
            pltpu.VMEM((ROWS, D), BF16),
            pltpu.VMEM((NX, NZ, NL, OWN, BW), BF16),
            pltpu.VMEM((NZ, NL, NX, OWN, D), BF16),
            pltpu.VMEM((1, OWN), BF16),
            pltpu.VMEM((ROWS, UNITS), BF16),
            pltpu.VMEM((NX, UNITS // NX, ROWS), F32),
            pltpu.VMEM((NX, UNITS // NX, ROWS), BF16),
            pltpu.VMEM((4, ROWS, 256), BF16),
            pltpu.VMEM((4, ROWS, 128), BF16),
            pltpu.VMEM((3, ROWS, 128), BF16),
            pltpu.VMEM((3, ROWS, 128), BF16),
            pltpu.VMEM((3, NZ, NL, OWN, CX), BF16),
            pltpu.VMEM((3, NZ, NL, OWN, CX), BF16),
            pltpu.VMEM((NZ, NL, OWN, CX), BF16),
            pltpu.VMEM((NL * NZ - 1, OWN, CX), BF16),
            pltpu.VMEM((NZ, NX, NL, OWN, D - CX), BF16),
            pltpu.VMEM((NZ - 1, NX, NL, OWN, D - CX), BF16),
            pltpu.VMEM((NX, NL, OWN, D - CX), BF16),
            pltpu.VMEM((NX * NL - 1, OWN, D - CX), BF16),
            pltpu.SemaphoreType.DMA((150,)),
            pltpu.SemaphoreType.DMA((150,)),
            pltpu.SemaphoreType.DMA((5,)),
        ],
        compiler_params=pltpu.CompilerParams(
            collective_id=0, has_side_effects=True, vmem_limit_bytes=60 * 1024 * 1024
        ),
        cost_estimate=pl.CostEstimate(flops=2147483648, bytes_accessed=8388608, transcendentals=262144),
    )(tokens, cotangent, w_in, b_in.reshape(1, OWN), w_out)


def solution(mesh):
    in_specs = (
        P("dp", "tensor"),
        P("dp", "tensor"),
        P(("dp", "tensor"), None),
        P(("dp", "tensor")),
        P(("dp", "tensor"), None),
    )
    out_specs = (P("dp", "tensor"), P(("dp", "tensor"), None))
    return jax.shard_map(
        on_device, mesh=mesh, in_specs=in_specs, out_specs=out_specs, check_vma=False
    )
```

```python
import math

import jax
import jax.numpy as jnp
from jax import lax
from jax.experimental import pallas as pl
from jax.experimental.pallas import tpu as pltpu
from jax.sharding import PartitionSpec as P

MESH = pl.DeviceIdType.MESH
BF16, F32 = jnp.bfloat16, jnp.float32
NX, NL, NZ, NY = 4, 2, 8, 4
ROWS, D, OWN = 512, 1024, 8
UNITS = NX * NL * NZ * OWN
BW = D + 128
HALF = ROWS // 2
CX = 768
CH = CX // 2


def gelu_parts(value):
    coeff = 0.7978845608
    square = value * value
    tangent = jnp.tanh(coeff * value * (1.0 + 0.044715 * square))
    half = 0.5 * (1.0 + tangent)
    slope = half + 0.5 * value * (1.0 - tangent * tangent) * coeff * (1.0 + 3.0 * 0.044715 * square)
    return value * half, slope


def kernel(
    tok_in, cot_in, win_in, b_in, wout_in, mixed_out, grad_out,
    tok, cot, w_i, w_o, b_own, act, slope, dpre, mix_s, mix_r, mix_o, mix_in,
    g_s, g_r, g_p, g_q, h_s, h_r, h_p, h_q,
    send_sem, recv_sem, local_sem,
):
    d, t = lax.axis_index("dp"), lax.axis_index("tensor")
    x, yl, z = d // (NL * NZ), (d // NZ) % NL, d % NZ
    yh, c = t // 2, t % 2

    def peer(dx=0, dl=0, dz=0, dy=0, dc=0):
        px, pz, py = (x + dx + NX) % NX, (z + dz + NZ) % NZ, (yh + dy + NY) % NY
        return ((px * NL + (yl + dl) % NL) * NZ + pz, py * 2 + (c + dc) % 2)

    count = [0]
    started = []

    def send(src, dst, to):
        k = count[0]
        count[0] += 1
        copy = pltpu.make_async_remote_copy(
            src_ref=src, dst_ref=dst, send_sem=send_sem.at[k], recv_sem=recv_sem.at[k],
            device_id=to, device_id_type=MESH,
        )
        copy.start()
        started.append(copy)
        return copy

    near_x = [dict(dx=i) for i in (2, 1, -1)]
    near_z = [dict(dz=i) for i in (1, -1, 2, -2, 3, -3, 4)]
    near_xl = [dict(dx=i, dl=l) for i in (2, 1, -1, 0) for l in (1, 0) if (i, l) != (0, 0)]
    near_lz = [dict(dz=i, dl=l) for i in (4, 3, -3, 2, -2, 1, -1, 0) for l in (1, 0) if (i, l) != (0, 0)]
    near_y = [dict(dy=i) for i in (2, 1, -1)]
    sibling, partner = dict(dc=1), dict(dl=1)

    barrier = pltpu.get_barrier_semaphore()
    greeted = near_lz + [p for p in near_xl if p["dx"]] + near_y + [sibling]
    for p in greeted:
        pl.semaphore_signal(barrier, inc=1, device_id=peer(**p), device_id_type=MESH)

    own_columns = pl.ds(pl.multiple_of(t * 128, 128), 128)
    local = [
        pltpu.make_async_copy(src, dst, local_sem.at[k])
        for k, (src, dst) in enumerate((
            (b_in, b_own),
            (win_in, w_i.at[x, z, yl, :, pl.ds(0, D)]),
            (wout_in, w_o.at[z, yl, x]),
            (tok_in, tok.at[:, own_columns]),
            (cot_in, cot.at[:, own_columns]),
        ))
    ]
    for copy in local:
        copy.start()
    local[0].wait()
    eye = lax.broadcasted_iota(jnp.int32, (OWN, OWN), 0) == lax.broadcasted_iota(jnp.int32, (OWN, OWN), 1)
    bias = jnp.broadcast_to(b_own[...].astype(F32), (OWN, OWN))
    bias = jnp.sum(jnp.where(eye, bias, 0.0), axis=1, keepdims=True)
    w_i[x, z, yl, :, D:BW] = jnp.broadcast_to(bias, (OWN, 128)).astype(BF16)
    for copy in local[1:]:
        copy.wait()
    pl.semaphore_wait(barrier, len(greeted))

    def columns(dy, dc=0):
        py, pc = (yh + dy + NY) % NY, (c + dc) % 2
        return pl.ds(pl.multiple_of(py * 256 + pc * 128, 128), 128)

    top, bottom, whole = pl.ds(0, HALF), pl.ds(HALF, HALF), pl.ds(0, ROWS)

    def place(buf, rows, dy):
        return buf.at[rows, columns(dy)]

    def spread(buf):
        out = {}
        out["up_a"] = send(place(buf, top, 0), place(buf, top, 0), peer(dy=1))
        out["dn_b"] = send(place(buf, bottom, 0), place(buf, bottom, 0), peer(dy=-1))
        out["up_b"] = send(place(buf, bottom, 0), place(buf, bottom, 0), peer(dy=1))
        out["dn_a"] = send(place(buf, top, 0), place(buf, top, 0), peer(dy=-1))
        out["sib"] = []
        return out

    def pass_on(buf, out):
        out["up_a"].wait_recv()
        out["fw_a"] = send(place(buf, top, -1), place(buf, top, -1), peer(dy=1))
        out["dn_b"].wait_recv()
        out["fw_b"] = send(place(buf, bottom, 1), place(buf, bottom, 1), peer(dy=-1))

    def share(buf, out, near):
        if near:
            for key, dy in (("up_b", -1), ("dn_a", 1)):
                out[key].wait_recv()
                out["sib"].append(send(place(buf, whole, dy), place(buf, whole, dy), peer(**sibling)))
        else:
            for key, rows in (("fw_a", top), ("fw_b", bottom)):
                out[key].wait_recv()
                out["sib"].append(send(place(buf, rows, 2), place(buf, rows, 2), peer(**sibling)))

    def settle(out):
        for copy in out["sib"]:
            copy.wait_recv()

    def arrive(moves):
        for copy in moves:
            copy.wait_recv()

    def wi_to_z(l):
        return [send(w_i.at[x, z, l], w_i.at[x, z, l], peer(**p)) for p in near_z]

    def wi_to_x(dz):
        pz = (z + dz + NZ) % NZ
        return [send(w_i.at[x, pz], w_i.at[x, pz], peer(**p)) for p in near_x]

    def wo_to_x(l):
        return [send(w_o.at[z, l, x], w_o.at[z, l, x], peer(**p)) for p in near_x]

    def ring_step(step, half, before=None):
        l = (yl + half) % NL
        out = []
        for k, sign in enumerate((1, -1)):
            if before is not None:
                before[k].wait_recv()
            if step < NZ // 2 or k == half:
                pz = (z - sign * (step - 1) + NZ) % NZ
                out.append(send(w_o.at[pz, l], w_o.at[pz, l], peer(dz=sign)))
        return out

    wi_own = send(w_i.at[x, z, yl], w_i.at[x, z, yl], peer(**partner))
    wo_own = send(w_o.at[z, yl, x], w_o.at[z, yl, x], peer(**partner))
    wo_moves = wo_to_x(yl)
    wi_moves = wi_to_z(yl)
    tok_moves = spread(tok)
    wi_own.wait_recv()
    wi_more = wi_to_z(1 - yl)
    wi_second = wi_to_x(0)
    wo_own.wait_recv()
    wo_more = wo_to_x(1 - yl)

    def relay(*dzs):
        out = []
        for dz in dzs:
            k = [p["dz"] for p in near_z].index(-dz if dz != 4 else 4)
            wi_moves[k].wait_recv()
            wi_more[k].wait_recv()
            out += wi_to_x(dz)
        return out

    arrive(wo_moves)
    ring = [ring_step(1, 0), None]
    wi_second += relay(1, -1)
    cot_moves = spread(cot)
    for buf, moves in ((tok, tok_moves), (cot, cot_moves)):
        moves['sib'].append(send(place(buf, whole, 0), place(buf, whole, 0), peer(**sibling)))
    arrive(wo_more)
    ring[1] = ring_step(1, 1)
    wi_second += relay(2, -2)
    ring[0] = ring_step(2, 0, ring[0])
    wi_second += relay(3, -3)
    wi_second += relay(4)
    ring[1] = ring_step(2, 1, ring[1])
    pass_on(tok, tok_moves)
    ring[0] = ring_step(3, 0, ring[0])
    ring[1] = ring_step(3, 1, ring[1])
    pass_on(cot, cot_moves)
    ring[0] = ring_step(4, 0, ring[0])
    ring[1] = ring_step(4, 1, ring[1])
    share(tok, tok_moves, True)
    share(tok, tok_moves, False)
    share(cot, cot_moves, True)
    arrive(wi_second)
    settle(tok_moves)

    last = (((1,), (1,)), ((), ()))

    def rows_of(value):
        return value.astype(F32).reshape(-1, value.shape[-1]).astype(BF16)

    for j in range(2):
        rows = rows_of(w_i[2 * j : 2 * j + 2])
        bias = rows[:, D:BW].astype(F32)
        pre = lax.dot_general(rows[:, 0:D], tok[...], last, preferred_element_type=F32)
        pre = pre + jnp.concatenate([bias] * (ROWS // 128), axis=1)
        value, grade = gelu_parts(pre)
        act[:, j * 256 : (j + 1) * 256] = value.astype(BF16).T
        slope[2 * j] = grade[0:128]
        slope[2 * j + 1] = grade[128:256]
    arrive(ring[0] + ring[1])
    pair = []
    for k, dy in enumerate((2, 1, -1, 0)):
        span = pl.ds(pl.multiple_of(((yh + dy + NY) % NY) * 256, 256), 256)
        weights = jnp.concatenate([rows_of(w_o[:, :, px, :, span]) for px in range(NX)], axis=0)
        term = jnp.dot(act[...], weights, preferred_element_type=F32)
        mix_s[k] = term.astype(BF16)
        theirs = pl.ds(pl.multiple_of((1 - c) * 128, 128), 128)
        pair.append(send(mix_s.at[k, :, theirs], mix_r.at[k], peer(**sibling)))
    share(cot, cot_moves, False)
    mine = pl.ds(pl.multiple_of(c * 128, 128), 128)
    out_moves = []
    for k, p in enumerate(near_y):
        pair[k].wait_recv()
        mix_o[k] = (mix_s[k, :, mine].astype(F32) + mix_r[k].astype(F32)).astype(BF16)
        out_moves.append(send(mix_o.at[k], mix_in.at[k], peer(**p)))
    settle(cot_moves)

    def units_of(px):
        dact = lax.dot_general(rows_of(w_o[:, :, px]), cot[...], last, preferred_element_type=F32)
        value = (dact * slope[px]).astype(BF16)
        dpre[px] = value
        return jnp.dot(value, tok[:, 0:CX], preferred_element_type=F32).reshape(NZ, NL, OWN, CX)

    x_moves = [[], []]
    for k, p in enumerate(near_x):
        value = units_of((x + p["dx"] + NX) % NX).astype(BF16)
        for h in range(2):
            g_s[h, k] = value[..., h * CH : (h + 1) * CH]
        x_moves[0].append(send(g_s.at[0, k], g_r.at[0, k], peer(**p)))
    for k, p in enumerate(near_x):
        x_moves[1].append(send(g_s.at[1, k], g_r.at[1, k], peer(**p)))
    own = units_of(x)
    rest = jnp.dot(dpre[...].reshape(UNITS, ROWS), tok[:, CX:D], preferred_element_type=F32)
    for px in range(NX):
        h_s[:, px] = rest[px * 128 : (px + 1) * 128].reshape(NZ, NL, OWN, D - CX).astype(BF16)
    far_z = near_z[::-1]
    z_moves = [send(h_s.at[(z + p["dz"] + NZ) % NZ], h_r.at[k], peer(**p)) for k, p in enumerate(far_z)]


    def over_lz(h):
        arrive(x_moves[h])
        total = own[..., h * CH : (h + 1) * CH] + (g_r[h, 0].astype(F32) + g_r[h, 1].astype(F32) + g_r[h, 2].astype(F32))
        g_p[h] = total.astype(BF16)
        moves = []
        for k, p in enumerate(near_lz):
            block = g_p.at[h, (z + p["dz"] + NZ) % NZ, (yl + p["dl"]) % NL]
            moves.append(send(block, g_q.at[h, k], peer(**p)))
        return moves

    lz_moves = [over_lz(0)]
    side = h_s[z].astype(F32)
    for k, copy in enumerate(z_moves):
        copy.wait_recv()
        side = side + h_r[k].astype(F32)
    h_p[...] = side.astype(BF16)
    xl_moves = []
    for k, p in enumerate(near_xl):
        block = h_p.at[(x + p["dx"] + NX) % NX, (yl + p["dl"]) % NL]
        xl_moves.append(send(block, h_q.at[k], peer(**p)))
    lz_moves.append(over_lz(1))

    pair[3].wait_recv()
    result = mix_s[3, :, mine].astype(F32) + mix_r[3].astype(F32)
    for k in range(3):
        out_moves[k].wait_recv()
        result = result + mix_in[k].astype(F32)
    mixed_out[...] = result.astype(BF16)

    scale = 1.0 / math.sqrt(ROWS * NX * NL * NZ)
    total = h_p[x, yl].astype(F32)
    for k in range(len(near_xl)):
        xl_moves[k].wait_recv()
        total = total + h_q[k].astype(F32)
    grad_out[:, CX:D] = total * scale
    for h in range(2):
        total = g_p[h, z, yl].astype(F32)
        for k in range(len(near_lz)):
            lz_moves[h][k].wait_recv()
            total = total + g_q[h, k].astype(F32)
        grad_out[:, h * CH : (h + 1) * CH] = total * scale

    for copy in started:
        copy.wait_send()


def on_device(tokens, cotangent, w_in, b_in, w_out):
    vmem = pl.BlockSpec(memory_space=pltpu.VMEM)
    return pl.pallas_call(
        kernel,
        out_shape=(
            jax.ShapeDtypeStruct((ROWS, 128), BF16),
            jax.ShapeDtypeStruct((OWN, D), F32),
        ),
        in_specs=[pl.BlockSpec(memory_space=pltpu.HBM)] * 5,
        out_specs=(vmem, vmem),
        scratch_shapes=[
            pltpu.VMEM((ROWS, D), BF16),
            pltpu.VMEM((ROWS, D), BF16),
            pltpu.VMEM((NX, NZ, NL, OWN, BW), BF16),
            pltpu.VMEM((NZ, NL, NX, OWN, D), BF16),
            pltpu.VMEM((1, OWN), BF16),
            pltpu.VMEM((ROWS, UNITS), BF16),
            pltpu.VMEM((NX, UNITS // NX, ROWS), F32),
            pltpu.VMEM((NX, UNITS // NX, ROWS), BF16),
            pltpu.VMEM((4, ROWS, 256), BF16),
            pltpu.VMEM((4, ROWS, 128), BF16),
            pltpu.VMEM((3, ROWS, 128), BF16),
            pltpu.VMEM((3, ROWS, 128), BF16),
            pltpu.VMEM((2, 3, NZ, NL, OWN, CH), BF16),
            pltpu.VMEM((2, 3, NZ, NL, OWN, CH), BF16),
            pltpu.VMEM((2, NZ, NL, OWN, CH), BF16),
            pltpu.VMEM((2, NL * NZ - 1, OWN, CH), BF16),
            pltpu.VMEM((NZ, NX, NL, OWN, D - CX), BF16),
            pltpu.VMEM((NZ - 1, NX, NL, OWN, D - CX), BF16),
            pltpu.VMEM((NX, NL, OWN, D - CX), BF16),
            pltpu.VMEM((NX * NL - 1, OWN, D - CX), BF16),
            pltpu.SemaphoreType.DMA((170,)),
            pltpu.SemaphoreType.DMA((170,)),
            pltpu.SemaphoreType.DMA((5,)),
        ],
        compiler_params=pltpu.CompilerParams(
            collective_id=0, has_side_effects=True, vmem_limit_bytes=60 * 1024 * 1024
        ),
        cost_estimate=pl.CostEstimate(flops=2147483648, bytes_accessed=8388608, transcendentals=262144),
    )(tokens, cotangent, w_in, b_in.reshape(1, OWN), w_out)


def solution(mesh):
    in_specs = (
        P("dp", "tensor"),
        P("dp", "tensor"),
        P(("dp", "tensor"), None),
        P(("dp", "tensor")),
        P(("dp", "tensor"), None),
    )
    out_specs = (P("dp", "tensor"), P(("dp", "tensor"), None))
    return jax.shard_map(
        on_device, mesh=mesh, in_specs=in_specs, out_specs=out_specs, check_vma=False
    )
```

```python
import math

import jax
import jax.numpy as jnp
from jax import lax
from jax.experimental import pallas as pl
from jax.experimental.pallas import tpu as pltpu
from jax.sharding import PartitionSpec as P

MESH = pl.DeviceIdType.MESH
BF16, F32 = jnp.bfloat16, jnp.float32
NX, NL, NZ, NY = 4, 2, 8, 4
ROWS, D, OWN = 512, 1024, 8
UNITS = NX * NL * NZ * OWN
BW = D + 128
HALF = ROWS // 2
CX = 768
CH = CX // 2


def gelu_parts(value):
    coeff = 0.7978845608
    square = value * value
    tangent = jnp.tanh(coeff * value * (1.0 + 0.044715 * square))
    half = 0.5 * (1.0 + tangent)
    slope = half + 0.5 * value * (1.0 - tangent * tangent) * coeff * (1.0 + 3.0 * 0.044715 * square)
    return value * half, slope


def kernel(
    tok_in, cot_in, win_in, b_in, wout_in, mixed_out, grad_out,
    tok, cot, w_i, w_o, b_own, act, slope, dpre, mix_s, mix_r, mix_o, mix_in,
    g_s, g_r, g_p, g_q, h_s, h_r, h_p, h_q,
    send_sem, recv_sem, local_sem,
):
    d, t = lax.axis_index("dp"), lax.axis_index("tensor")
    x, yl, z = d // (NL * NZ), (d // NZ) % NL, d % NZ
    yh, c = t // 2, t % 2

    def peer(dx=0, dl=0, dz=0, dy=0, dc=0):
        px, pz, py = (x + dx + NX) % NX, (z + dz + NZ) % NZ, (yh + dy + NY) % NY
        return ((px * NL + (yl + dl) % NL) * NZ + pz, py * 2 + (c + dc) % 2)

    count = [0]
    started = []

    def send(src, dst, to):
        k = count[0]
        count[0] += 1
        copy = pltpu.make_async_remote_copy(
            src_ref=src, dst_ref=dst, send_sem=send_sem.at[k], recv_sem=recv_sem.at[k],
            device_id=to, device_id_type=MESH,
        )
        copy.start()
        started.append(copy)
        return copy

    near_x = [dict(dx=i) for i in (2, 1, -1)]
    near_z = [dict(dz=i) for i in (1, -1, 2, -2, 3, -3, 4)]
    near_xl = [dict(dx=i, dl=l) for i in (2, 1, -1, 0) for l in (1, 0) if (i, l) != (0, 0)]
    near_lz = [dict(dz=i, dl=l) for i in (4, 3, -3, 2, -2, 1, -1, 0) for l in (1, 0) if (i, l) != (0, 0)]
    near_y = [dict(dy=i) for i in (2, 1, -1)]
    sibling, partner = dict(dc=1), dict(dl=1)

    barrier = pltpu.get_barrier_semaphore()
    greeted = near_lz + [p for p in near_xl if p["dx"]] + near_y + [sibling]
    for p in greeted:
        pl.semaphore_signal(barrier, inc=1, device_id=peer(**p), device_id_type=MESH)

    own_columns = pl.ds(pl.multiple_of(t * 128, 128), 128)
    local = [
        pltpu.make_async_copy(src, dst, local_sem.at[k])
        for k, (src, dst) in enumerate((
            (b_in, b_own),
            (win_in, w_i.at[x, z, yl, :, pl.ds(0, D)]),
            (wout_in, w_o.at[z, yl, x]),
            (tok_in, tok.at[:, own_columns]),
            (cot_in, cot.at[:, own_columns]),
        ))
    ]
    for copy in local:
        copy.start()
    local[0].wait()
    eye = lax.broadcasted_iota(jnp.int32, (OWN, OWN), 0) == lax.broadcasted_iota(jnp.int32, (OWN, OWN), 1)
    bias = jnp.broadcast_to(b_own[...].astype(F32), (OWN, OWN))
    bias = jnp.sum(jnp.where(eye, bias, 0.0), axis=1, keepdims=True)
    w_i[x, z, yl, :, D:BW] = jnp.broadcast_to(bias, (OWN, 128)).astype(BF16)
    for copy in local[1:]:
        copy.wait()
    pl.semaphore_wait(barrier, len(greeted))

    def columns(dy, dc=0):
        py, pc = (yh + dy + NY) % NY, (c + dc) % 2
        return pl.ds(pl.multiple_of(py * 256 + pc * 128, 128), 128)

    top, bottom, whole = pl.ds(0, HALF), pl.ds(HALF, HALF), pl.ds(0, ROWS)

    def place(buf, rows, dy):
        return buf.at[rows, columns(dy)]

    def spread(buf):
        out = {}
        out["up_a"] = send(place(buf, top, 0), place(buf, top, 0), peer(dy=1))
        out["dn_b"] = send(place(buf, bottom, 0), place(buf, bottom, 0), peer(dy=-1))
        out["up_b"] = send(place(buf, bottom, 0), place(buf, bottom, 0), peer(dy=1))
        out["dn_a"] = send(place(buf, top, 0), place(buf, top, 0), peer(dy=-1))
        out["sib"] = []
        return out

    def pass_on(buf, out):
        out["up_a"].wait_recv()
        out["fw_a"] = send(place(buf, top, -1), place(buf, top, -1), peer(dy=1))
        out["dn_b"].wait_recv()
        out["fw_b"] = send(place(buf, bottom, 1), place(buf, bottom, 1), peer(dy=-1))

    def share(buf, out, near):
        if near:
            for key, dy in (("up_b", -1), ("dn_a", 1)):
                out[key].wait_recv()
                out["sib"].append(send(place(buf, whole, dy), place(buf, whole, dy), peer(**sibling)))
        else:
            for key, rows in (("fw_a", top), ("fw_b", bottom)):
                out[key].wait_recv()
                out["sib"].append(send(place(buf, rows, 2), place(buf, rows, 2), peer(**sibling)))

    def settle(out):
        for copy in out["sib"]:
            copy.wait_recv()

    def arrive(moves):
        for copy in moves:
            copy.wait_recv()

    def wi_to_z(l):
        return [send(w_i.at[x, z, l], w_i.at[x, z, l], peer(**p)) for p in near_z]

    def wi_to_x(dz, l):
        block = w_i.at[x, (z + dz + NZ) % NZ, l]
        return [send(block, block, peer(**p)) for p in near_x]

    def wo_to_x(l):
        return [send(w_o.at[z, l, x], w_o.at[z, l, x], peer(**p)) for p in near_x]

    def ring_step(step, half, before=None):
        l = (yl + half) % NL
        out = []
        for k, sign in enumerate((1, -1)):
            if before is not None:
                before[k].wait_recv()
            if step < NZ // 2 or k == half:
                pz = (z - sign * (step - 1) + NZ) % NZ
                out.append(send(w_o.at[pz, l], w_o.at[pz, l], peer(dz=sign)))
        return out

    wi_own = send(w_i.at[x, z, yl], w_i.at[x, z, yl], peer(**partner))
    wo_own = send(w_o.at[z, yl, x], w_o.at[z, yl, x], peer(**partner))
    wo_moves = wo_to_x(yl)
    wi_second = wi_to_x(0, yl)
    wi_moves = wi_to_z(yl)
    tok_moves = spread(tok)
    wi_own.wait_recv()
    wi_second += wi_to_x(0, 1 - yl)
    wi_more = wi_to_z(1 - yl)
    wo_own.wait_recv()
    wo_more = wo_to_x(1 - yl)

    def relay(moves, l, *dzs):
        out = []
        for dz in dzs:
            moves[[p["dz"] for p in near_z].index(-dz if dz != 4 else 4)].wait_recv()
            out += wi_to_x(dz, l)
        return out

    arrive(wo_moves)
    ring = [ring_step(1, 0), None]
    wi_second += relay(wi_moves, yl, 1, -1)
    arrive(wo_more)
    ring[1] = ring_step(1, 1)
    wi_second += relay(wi_moves, yl, 2, -2)
    cot_moves = spread(cot)
    for buf, moves in ((tok, tok_moves), (cot, cot_moves)):
        moves["sib"].append(send(place(buf, whole, 0), place(buf, whole, 0), peer(**sibling)))
    ring[0] = ring_step(2, 0, ring[0])
    wi_second += relay(wi_moves, yl, 3, -3)
    wi_second += relay(wi_moves, yl, 4)
    ring[1] = ring_step(2, 1, ring[1])
    wi_second += relay(wi_more, 1 - yl, 1, -1)
    wi_second += relay(wi_more, 1 - yl, 2, -2)
    pass_on(tok, tok_moves)
    ring[0] = ring_step(3, 0, ring[0])
    wi_second += relay(wi_more, 1 - yl, 3, -3)
    wi_second += relay(wi_more, 1 - yl, 4)
    ring[1] = ring_step(3, 1, ring[1])
    share(tok, tok_moves, True)
    pass_on(cot, cot_moves)
    ring[0] = ring_step(4, 0, ring[0])
    ring[1] = ring_step(4, 1, ring[1])
    share(tok, tok_moves, False)
    share(cot, cot_moves, True)
    arrive(wi_second)
    settle(tok_moves)

    last = (((1,), (1,)), ((), ()))

    def rows_of(value):
        return value.astype(F32).reshape(-1, value.shape[-1]).astype(BF16)

    for j in range(2):
        rows = rows_of(w_i[2 * j : 2 * j + 2])
        bias = rows[:, D:BW].astype(F32)
        pre = lax.dot_general(rows[:, 0:D], tok[...], last, preferred_element_type=F32)
        pre = pre + jnp.concatenate([bias] * (ROWS // 128), axis=1)
        value, grade = gelu_parts(pre)
        act[:, j * 256 : (j + 1) * 256] = value.astype(BF16).T
        slope[2 * j] = grade[0:128]
        slope[2 * j + 1] = grade[128:256]
    arrive(ring[0] + ring[1])
    pair = []
    for k, dy in enumerate((2, 1, -1, 0)):
        span = pl.ds(pl.multiple_of(((yh + dy + NY) % NY) * 256, 256), 256)
        weights = jnp.concatenate([rows_of(w_o[:, :, px, :, span]) for px in range(NX)], axis=0)
        term = jnp.dot(act[...], weights, preferred_element_type=F32)
        mix_s[k] = term.astype(BF16)
        theirs = pl.ds(pl.multiple_of((1 - c) * 128, 128), 128)
        pair.append(send(mix_s.at[k, :, theirs], mix_r.at[k], peer(**sibling)))
    share(cot, cot_moves, False)
    mine = pl.ds(pl.multiple_of(c * 128, 128), 128)
    out_moves = []
    for k, p in enumerate(near_y):
        pair[k].wait_recv()
        mix_o[k] = (mix_s[k, :, mine].astype(F32) + mix_r[k].astype(F32)).astype(BF16)
        out_moves.append(send(mix_o.at[k], mix_in.at[k], peer(**p)))
    settle(cot_moves)

    def units_of(px):
        dact = lax.dot_general(rows_of(w_o[:, :, px]), cot[...], last, preferred_element_type=F32)
        value = (dact * slope[px]).astype(BF16)
        dpre[px] = value
        return jnp.dot(value, tok[:, 0:CX], preferred_element_type=F32).reshape(NZ, NL, OWN, CX)

    x_moves = [[], []]
    for k, p in enumerate(near_x):
        value = units_of((x + p["dx"] + NX) % NX).astype(BF16)
        for h in range(2):
            g_s[h, k] = value[..., h * CH : (h + 1) * CH]
        x_moves[0].append(send(g_s.at[0, k], g_r.at[0, k], peer(**p)))
    for k, p in enumerate(near_x):
        x_moves[1].append(send(g_s.at[1, k], g_r.at[1, k], peer(**p)))
    own = units_of(x)
    rest = jnp.dot(dpre[...].reshape(UNITS, ROWS), tok[:, CX:D], preferred_element_type=F32)
    for px in range(NX):
        h_s[:, px] = rest[px * 128 : (px + 1) * 128].reshape(NZ, NL, OWN, D - CX).astype(BF16)
    far_z = near_z[::-1]
    z_moves = [send(h_s.at[(z + p["dz"] + NZ) % NZ], h_r.at[k], peer(**p)) for k, p in enumerate(far_z)]


    def over_lz(h):
        arrive(x_moves[h])
        total = own[..., h * CH : (h + 1) * CH] + (g_r[h, 0].astype(F32) + g_r[h, 1].astype(F32) + g_r[h, 2].astype(F32))
        g_p[h] = total.astype(BF16)
        moves = []
        for k, p in enumerate(near_lz):
            block = g_p.at[h, (z + p["dz"] + NZ) % NZ, (yl + p["dl"]) % NL]
            moves.append(send(block, g_q.at[h, k], peer(**p)))
        return moves

    lz_moves = [over_lz(0)]
    side = h_s[z].astype(F32)
    for k, copy in enumerate(z_moves):
        copy.wait_recv()
        side = side + h_r[k].astype(F32)
    h_p[...] = side.astype(BF16)
    xl_moves = []
    for k, p in enumerate(near_xl):
        block = h_p.at[(x + p["dx"] + NX) % NX, (yl + p["dl"]) % NL]
        xl_moves.append(send(block, h_q.at[k], peer(**p)))
    lz_moves.append(over_lz(1))

    pair[3].wait_recv()
    result = mix_s[3, :, mine].astype(F32) + mix_r[3].astype(F32)
    for k in range(3):
        out_moves[k].wait_recv()
        result = result + mix_in[k].astype(F32)
    mixed_out[...] = result.astype(BF16)

    scale = 1.0 / math.sqrt(ROWS * NX * NL * NZ)
    total = h_p[x, yl].astype(F32)
    for k in range(len(near_xl)):
        xl_moves[k].wait_recv()
        total = total + h_q[k].astype(F32)
    grad_out[:, CX:D] = total * scale
    for h in range(2):
        total = g_p[h, z, yl].astype(F32)
        for k in range(len(near_lz)):
            lz_moves[h][k].wait_recv()
            total = total + g_q[h, k].astype(F32)
        grad_out[:, h * CH : (h + 1) * CH] = total * scale

    for copy in started:
        copy.wait_send()


def on_device(tokens, cotangent, w_in, b_in, w_out):
    vmem = pl.BlockSpec(memory_space=pltpu.VMEM)
    return pl.pallas_call(
        kernel,
        out_shape=(
            jax.ShapeDtypeStruct((ROWS, 128), BF16),
            jax.ShapeDtypeStruct((OWN, D), F32),
        ),
        in_specs=[pl.BlockSpec(memory_space=pltpu.HBM)] * 5,
        out_specs=(vmem, vmem),
        scratch_shapes=[
            pltpu.VMEM((ROWS, D), BF16),
            pltpu.VMEM((ROWS, D), BF16),
            pltpu.VMEM((NX, NZ, NL, OWN, BW), BF16),
            pltpu.VMEM((NZ, NL, NX, OWN, D), BF16),
            pltpu.VMEM((1, OWN), BF16),
            pltpu.VMEM((ROWS, UNITS), BF16),
            pltpu.VMEM((NX, UNITS // NX, ROWS), F32),
            pltpu.VMEM((NX, UNITS // NX, ROWS), BF16),
            pltpu.VMEM((4, ROWS, 256), BF16),
            pltpu.VMEM((4, ROWS, 128), BF16),
            pltpu.VMEM((3, ROWS, 128), BF16),
            pltpu.VMEM((3, ROWS, 128), BF16),
            pltpu.VMEM((2, 3, NZ, NL, OWN, CH), BF16),
            pltpu.VMEM((2, 3, NZ, NL, OWN, CH), BF16),
            pltpu.VMEM((2, NZ, NL, OWN, CH), BF16),
            pltpu.VMEM((2, NL * NZ - 1, OWN, CH), BF16),
            pltpu.VMEM((NZ, NX, NL, OWN, D - CX), BF16),
            pltpu.VMEM((NZ - 1, NX, NL, OWN, D - CX), BF16),
            pltpu.VMEM((NX, NL, OWN, D - CX), BF16),
            pltpu.VMEM((NX * NL - 1, OWN, D - CX), BF16),
            pltpu.SemaphoreType.DMA((200,)),
            pltpu.SemaphoreType.DMA((200,)),
            pltpu.SemaphoreType.DMA((5,)),
        ],
        compiler_params=pltpu.CompilerParams(
            collective_id=0, has_side_effects=True, vmem_limit_bytes=60 * 1024 * 1024
        ),
        cost_estimate=pl.CostEstimate(flops=2147483648, bytes_accessed=8388608, transcendentals=262144),
    )(tokens, cotangent, w_in, b_in.reshape(1, OWN), w_out)


def solution(mesh):
    in_specs = (
        P("dp", "tensor"),
        P("dp", "tensor"),
        P(("dp", "tensor"), None),
        P(("dp", "tensor")),
        P(("dp", "tensor"), None),
    )
    out_specs = (P("dp", "tensor"), P(("dp", "tensor"), None))
    return jax.shard_map(
        on_device, mesh=mesh, in_specs=in_specs, out_specs=out_specs, check_vma=False
    )
```
